512 devices in a mesh: seq: 64 (over y, z), head: 8 (over x, core).
Axes of the slice: x: 4, y: 4, z: 16, core: 2. Of those that a mesh axis runs over, the one named last changes fastest.
Arguments:
- queries: bfloat16 [128, 4096], P(None, 'head'), may hold values from -400 to 400
- keys: bfloat16 [16384, 1024], P('seq', 'head'), may hold values from -6 to 6
- values: bfloat16 [16384, 1024], P('seq', 'head'), may hold values from -6 to 6
- householder: bfloat16 [16384, 1024], P('seq', 'head'), may hold values from -6 to 6
- out_proj: bfloat16 [4096, 4096], P('head', 'seq'), may hold values from -0.09375 to 0.09375
Outputs:
- mixed: bfloat16 [128, 4096], P('head', 'seq')
The draws below stay inside these ranges and needn't reach their ends.
All inputs are finite; a program needn't handle non-finite values.
Results may differ from the reference program's by a relative error of at most 0.02.
Values may be sent and summed in bfloat16 or wider, within the bound.
A program may use at most 64 MiB of HBM per device.

```python
import jax
import jax.numpy as jnp
from jax import lax

HEAD = 128
GROUP = 4
BLOCK = 64
QUERIES = 128
KV = 8
D = 4096
CTX = 16384


def draw_queries(key, part):
    normal_vals = jnp.clip(jax.random.normal(key, (QUERIES, D), jnp.float32), -6.0, 6.0)
    return normal_vals.astype(jnp.bfloat16)


def block_levels(stream_key, extent, shards, smallest, top_value):
    def one(position, blocks):
        steps = jax.random.uniform(jax.random.fold_in(jax.random.fold_in(stream_key, 6), position), (blocks,), jnp.float32, smallest / len(shards), top_value / len(shards))
        return jnp.repeat(jnp.exp(steps), extent[position] // blocks).reshape((-1,) + (1,) * (len(extent) - position - 1))

    level = one(*shards[0])
    for cut in shards[1:]:
        level = level * one(*cut)
    return level


def normal_values(rng, shape, deviation, limit, cuts=(), kind=jnp.bfloat16):
    factor_of = block_levels(rng, shape, cuts, -0.22, 0.18) if cuts else 1.0
    entries = jax.random.normal(rng, shape, jnp.float32) * deviation * factor_of
    return jnp.minimum(jnp.maximum(entries, -limit), limit).astype(kind)


def setup_inputs(seed: int = 0) -> dict:
    seeds = jax.random.split(jax.random.key(seed), 6)
    queries = draw_queries(jax.random.fold_in(seeds[5], 71), 0)
    keys = normal_values(seeds[1], (CTX, KV * HEAD), 1.0, 6.0, ((0, 64), (1, 8)))
    values = normal_values(seeds[2], (CTX, KV * HEAD), 1.0, 6.0, ((0, 64), (1, 8)))
    householder = normal_values(seeds[3], (CTX, KV * HEAD), 1.0, 6.0, ((0, 64), (1, 8)))
    out_proj = normal_values(seeds[4], (D, D), D ** -0.5, 0.09375, ((0, 8), (1, 64)))
    return {"queries": queries, "keys": keys, "values": values, "householder": householder, "out_proj": out_proj}


def unit_rows(raw_vecs):
    return raw_vecs * lax.rsqrt(lax.optimization_barrier(jnp.sum(raw_vecs * raw_vecs, axis=-1, keepdims=True)) + 1e-06)

def span_forms(raw_vecs, keys_float):
    precise = lax.Precision.HIGHEST
    vectors = unit_rows(raw_vecs)
    block_len = vectors.shape[1]
    head_width = vectors.shape[2]
    row_ids = lax.broadcasted_iota(jnp.int32, (block_len, block_len), 0)
    col_ids = lax.broadcasted_iota(jnp.int32, (block_len, block_len), 1)
    gram = jnp.einsum('nad,nbd->nab', vectors, vectors, precision=precise)
    lower = jnp.where(row_ids > col_ids, gram, 0.0) + jnp.where(row_ids == col_ids, 0.5, 0.0)
    identity_block = jnp.broadcast_to(jnp.eye(block_len, dtype=jnp.float32), lower.shape)
    coeff = jax.scipy.linalg.solve_triangular(lower, identity_block, lower=True)
    identity_head = jnp.eye(head_width, dtype=jnp.float32)
    transition = identity_head - jnp.einsum('nad,nab,nbe->nde', vectors, coeff, vectors, precision=precise)
    inner = jnp.einsum('nbd,njd->nbj', vectors, keys_float, precision=precise)
    inner = jnp.where(row_ids > col_ids, inner, 0.0)
    mixing = jnp.einsum('nab,nbj->naj', coeff, inner, precision=precise)
    carried = keys_float - jnp.einsum('naj,nad->njd', mixing, vectors, precision=precise)
    return (transition, carried)

def carry_back(transition, carried, identity_head):
    precise = lax.Precision.HIGHEST

    def advance(running, span_item):
        factor, block_keys = span_item
        emitted = jnp.dot(block_keys, running.T, precision=precise)
        return (jnp.dot(running, factor, precision=precise), emitted)
    return lax.scan(advance, identity_head, (transition, carried), reverse=True)

def reference(queries, keys, values, householder, out_proj):
    precise = lax.Precision.HIGHEST
    columns = []
    blocks = CTX // BLOCK
    identity_head = jnp.eye(HEAD, dtype=jnp.float32)
    for kv_head in range(KV):
        lo_col = kv_head * HEAD
        raw_vecs = householder[:, lo_col:lo_col + HEAD].astype(jnp.float32).reshape(blocks, BLOCK, HEAD)
        keys_float = keys[:, lo_col:lo_col + HEAD].astype(jnp.float32).reshape(blocks, BLOCK, HEAD)
        transition, carried = span_forms(raw_vecs, keys_float)
        _, moved = carry_back(transition, carried, identity_head)
        moved = moved.reshape(CTX, HEAD)
        head_values = values[:, lo_col:lo_col + HEAD]
        for member in range(GROUP):
            q_col = (kv_head * GROUP + member) * HEAD
            query_rows = queries[:, q_col:q_col + HEAD].astype(jnp.float32)
            scores = jnp.dot(query_rows, moved.T, precision=precise) / jnp.sqrt(jnp.float32(HEAD))
            peak = lax.optimization_barrier(jnp.max(scores, axis=1, keepdims=True))
            expo = jnp.exp(scores - peak)
            totals = lax.optimization_barrier(jnp.sum(expo, axis=1))
            numerators = jnp.dot(expo.astype(jnp.bfloat16).astype(jnp.float32), head_values.astype(jnp.float32), preferred_element_type=jnp.float32)
            columns.append((numerators / totals[:, None]).astype(jnp.bfloat16))
    attention = jnp.concatenate(columns, axis=1)
    return jnp.dot(attention.astype(jnp.float32), out_proj.astype(jnp.float32), preferred_element_type=jnp.float32).astype(jnp.bfloat16)
```

```python
import jax
import jax.numpy as jnp
from jax import lax
from jax.experimental import pallas as pl
from jax.experimental.pallas import tpu as pltpu
from jax.sharding import PartitionSpec as P

F32 = jnp.float32
BF16 = jnp.bfloat16
MESH = pl.DeviceIdType.MESH
RADIX = 4
ROWS_Y = 4
ROWS_Z = 16
HEADS = 8
HEAD = 128
ML_ROWS = 16
SLAB = HEAD + ML_ROWS

NN = (((1,), (0,)), ((), ()))
NT = (((1,), (1,)), ((), ()))
TN = (((0,), (0,)), ((), ()))


def dot(a, b, dims=NN):
    return lax.dot_general(a, b, dims, preferred_element_type=F32)


def split(x):
    high = x.astype(BF16)
    return high, (x - high.astype(F32)).astype(BF16)


def dot3(a, b, dims=NN):
    return dot(a[0], b[0], dims) + (dot(a[0], b[1], dims) + dot(a[1], b[0], dims))


def parts3(x):
    first = x.astype(BF16).astype(F32)
    rest = x - first
    second = rest.astype(BF16).astype(F32)
    return first, second, rest - second


def local_kernel(keys_ref, house_ref, trans_ref, carried_ref):
    raw = house_ref[...].astype(F32)
    vectors = raw * lax.rsqrt(jnp.sum(raw * raw, axis=1, keepdims=True) + 1e-06)
    count = vectors.shape[0]
    vec = split(vectors)
    keys = keys_ref[...]
    rows = lax.broadcasted_iota(jnp.int32, (count, count), 0)
    cols = lax.broadcasted_iota(jnp.int32, (count, count), 1)
    gram = dot3(vec, vec, NT)
    strict = jnp.where(rows < cols, gram, 0.0)
    pair = (rows | 1) == (cols | 1)
    inverse = jnp.where(rows == cols, 2.0, 0.0) - jnp.where(pair, 4.0 * strict, 0.0)
    size = 2
    while 2 * size < count:
        below = (rows & -(2 * size)) == (cols & -(2 * size))
        below = below & ((rows & size) != (cols & size))
        coupling = split(jnp.where(below, strict, 0.0))
        inv = split(inverse)
        inverse = inverse - dot3(split(dot3(inv, coupling)), inv)
        size *= 2
    coupling = split(jnp.where((rows & size) != (cols & size), strict, 0.0))
    inv = split(inverse)
    half = dot3(inv, vec)
    weights = split(half - dot3(inv, split(dot3(coupling, split(half)))))
    eye_rows = lax.broadcasted_iota(jnp.int32, (HEAD, HEAD), 0)
    eye_cols = lax.broadcasted_iota(jnp.int32, (HEAD, HEAD), 1)
    identity = jnp.where(eye_rows == eye_cols, 1.0, 0.0)
    trans_high, trans_low = split(identity - dot3(weights, vec, TN))
    trans_ref[0] = trans_high
    trans_ref[1] = trans_low
    inner = dot(keys, vec[0], NT) + dot(keys, vec[1], NT)
    inner = split(jnp.where(rows < cols, inner, 0.0))
    carried_high, carried_low = split(keys.astype(F32) - dot3(inner, weights))
    carried_ref[0] = carried_high
    carried_ref[1] = carried_low


def chain(buf, last):
    products = [None] * RADIX
    running = (buf[RADIX - 1, 0], buf[RADIX - 1, 1])
    products[RADIX - 1] = running[0].astype(F32) + running[1].astype(F32)
    for i in range(RADIX - 2, last - 1, -1):
        products[i] = dot3(running, (buf[i, 0], buf[i, 1]))
        running = split(products[i])
    return products, running


def chosen(products, position):
    eye_rows = lax.broadcasted_iota(jnp.int32, (HEAD, HEAD), 0)
    eye_cols = lax.broadcasted_iota(jnp.int32, (HEAD, HEAD), 1)
    out = jnp.where(eye_rows == eye_cols, 1.0, 0.0)
    for i in range(RADIX - 1):
        out = jnp.where(position == i, products[i + 1], out)
    return out


def stat_rows(peak, total, rows):
    ids = lax.broadcasted_iota(jnp.int32, (rows, HEAD), 0)
    out = jnp.zeros((rows, HEAD), F32)
    for i, part in enumerate(parts3(peak) + parts3(total)):
        out = jnp.where(ids == i, part, out)
    return out


def remote_kernel(
    trans_ref, carried_ref, q_ref, v_ref, w_ref, o_ref,
    buf_a, buf_b, buf_y, slab_out, slab_in, part_out, part_in, att_z, att_y, mix_out, mix_in,
    sem_a, sem_b, sem_y, sem_sy, sem_sz, sem_gz, sem_gy, sem_h,
):
    seq = lax.axis_index("seq")
    head = lax.axis_index("head")
    y = lax.div(seq, ROWS_Z)
    z = lax.rem(seq, ROWS_Z)
    a = lax.div(z, RADIX)
    p = lax.rem(z, RADIX)
    started = []

    def y_peer(k):
        other = lax.rem(y + k, ROWS_Y)
        return other, (other * ROWS_Z + z, head)

    def z_peer(k):
        other = lax.rem(z + k, ROWS_Z)
        return other, (y * ROWS_Z + other, head)

    def a_peer(k):
        other = lax.rem(a + k, RADIX)
        return other, (y * ROWS_Z + other * RADIX + p, head)

    def p_peer(k):
        other = lax.rem(p + k, RADIX)
        return other, (y * ROWS_Z + a * RADIX + other, head)

    def head_peer(k):
        other = lax.rem(head + k, HEADS)
        return other, (seq, other)

    def exchange(peer, count, sems, source, target):
        copies = []
        for k in range(1, count):
            other, device = peer(k)
            copy = pltpu.make_async_remote_copy(
                src_ref=source(other), dst_ref=target,
                send_sem=sems.at[0, k], recv_sem=sems.at[1, k],
                device_id=device, device_id_type=MESH,
            )
            copy.start()
            copies.append(copy)
        started.extend(copies)
        return copies

    def arrived(copies):
        for copy in copies:
            copy.wait_recv()

    barrier = pltpu.get_barrier_semaphore()
    peers = 0
    for peer, count in ((z_peer, ROWS_Z), (y_peer, ROWS_Y), (head_peer, HEADS)):
        for k in range(1, count):
            pl.semaphore_signal(barrier, inc=1, device_id=peer(k)[1], device_id_type=MESH)
            peers += 1
    pl.semaphore_wait(barrier, peers)

    copies = exchange(p_peer, RADIX, sem_a, lambda other: trans_ref, buf_a.at[p])
    buf_a[p] = trans_ref[...]
    arrived(copies)
    products, full = chain(buf_a, 0)
    buf_b[a, 0] = full[0]
    buf_b[a, 1] = full[1]
    copies = exchange(a_peer, RADIX, sem_b, lambda other: buf_b.at[a], buf_b.at[a])
    after = split(chosen(products, p))
    arrived(copies)
    products, full = chain(buf_b, 0)
    buf_y[y, 0] = full[0]
    buf_y[y, 1] = full[1]
    copies = exchange(y_peer, ROWS_Y, sem_y, lambda other: buf_y.at[y], buf_y.at[y])
    after = split(dot3(split(chosen(products, a)), after))
    arrived(copies)
    products, _ = chain(buf_y, 1)
    suffix = split(dot3(split(chosen(products, y)), after))

    carried = (carried_ref[0], carried_ref[1])
    for h in range(RADIX):
        query = q_ref[:, h * HEAD:(h + 1) * HEAD]
        turned = split((dot(query, suffix[0]) + dot(query, suffix[1])) * (HEAD ** -0.5))
        scores = dot3(carried, turned, NT)
        peak = jnp.max(scores, axis=0, keepdims=True)
        expo = jnp.exp(scores - peak)
        total = jnp.sum(expo, axis=0, keepdims=True)
        numer = dot(v_ref[...], expo.astype(BF16), TN)
        slab_out[h, 0:HEAD, :] = numer.astype(BF16)
        slab_out[h, HEAD:SLAB, :] = stat_rows(peak, total, ML_ROWS).astype(BF16)

    copies = exchange(y_peer, ROWS_Y, sem_sy, lambda other: slab_out.at[other], slab_in.at[y])
    slab_in[y] = slab_out[y]
    arrived(copies)
    slabs = [slab_in[i].astype(F32) for i in range(ROWS_Y)]
    peaks = [s[HEAD:HEAD + 1] + s[HEAD + 1:HEAD + 2] + s[HEAD + 2:HEAD + 3] for s in slabs]
    totals = [s[HEAD + 3:HEAD + 4] + s[HEAD + 4:HEAD + 5] + s[HEAD + 5:HEAD + 6] for s in slabs]
    peak = jnp.maximum(jnp.maximum(peaks[0], peaks[1]), jnp.maximum(peaks[2], peaks[3]))
    factors = [jnp.exp(one - peak) for one in peaks]
    total = sum(f * t for f, t in zip(factors, totals))
    numer = sum(f * s[0:HEAD] for f, s in zip(factors, slabs))

    stats = jnp.broadcast_to(stat_rows(peak, total, 8)[None], (ROWS_Z, 8, HEAD))
    part_out[...] = jnp.concatenate([numer.reshape(ROWS_Z, 8, HEAD), stats], axis=1).astype(BF16)
    copies = exchange(z_peer, ROWS_Z, sem_sz, lambda other: part_out.at[other], part_in.at[z])
    part_in[z] = part_out[z]
    arrived(copies)
    parts = part_in[...].astype(F32)
    peaks = parts[:, 8:9] + parts[:, 9:10] + parts[:, 10:11]
    totals = parts[:, 11:12] + parts[:, 12:13] + parts[:, 13:14]
    factors = jnp.exp(peaks - jnp.max(peaks, axis=0, keepdims=True))
    total = jnp.sum(factors * totals, axis=0)
    numer = jnp.sum(factors * parts[:, 0:8], axis=0)
    mine = pl.ds(pl.multiple_of(z * 8, 8), 8)
    att_z[mine, :] = numer / total
    arrived(exchange(z_peer, ROWS_Z, sem_gz, lambda other: att_z.at[mine], att_z.at[mine]))
    att_y[y] = att_z[...].astype(BF16)
    arrived(exchange(y_peer, ROWS_Y, sem_gy, lambda other: att_y.at[y], att_y.at[y]))

    attention = att_y[...].reshape(RADIX * HEAD, HEAD)
    mixed = dot(attention, w_ref[...], TN)
    mix_out[...] = jnp.zeros(mix_out.shape, F32)
    mix_out[:, :, 0:mixed.shape[1]] = mixed.reshape(HEADS, HEAD // HEADS, mixed.shape[1])
    copies = exchange(head_peer, HEADS, sem_h, lambda other: mix_out.at[other], mix_in.at[head])
    mix_in[head] = mix_out[head]
    arrived(copies)
    o_ref[...] = jnp.sum(mix_in[...], axis=0)[:, 0:mixed.shape[1]].astype(BF16)
    for copy in started:
        copy.wait_send()


def on_device(queries, keys, values, householder, out_proj):
    count = keys.shape[0]
    vmem = pl.BlockSpec(memory_space=pltpu.VMEM)
    trans, carried = pl.pallas_call(
        local_kernel,
        out_shape=(
            jax.ShapeDtypeStruct((2, HEAD, HEAD), BF16),
            jax.ShapeDtypeStruct((2, count, HEAD), BF16),
        ),
        in_specs=[vmem] * 2,
        out_specs=(vmem, vmem),
        compiler_params=pltpu.CompilerParams(vmem_limit_bytes=32 * 1024 * 1024),
        name="local_transition",
    )(keys, householder)
    sems = [pltpu.SemaphoreType.DMA((2, n)) for n in (4, 4, 4, 4, 16, 16, 4, 8)]
    return pl.pallas_call(
        remote_kernel,
        out_shape=jax.ShapeDtypeStruct((HEAD // HEADS, out_proj.shape[1]), BF16),
        in_specs=[vmem] * 5,
        out_specs=vmem,
        scratch_shapes=[
            pltpu.VMEM((RADIX, 2, HEAD, HEAD), BF16),
            pltpu.VMEM((RADIX, 2, HEAD, HEAD), BF16),
            pltpu.VMEM((RADIX, 2, HEAD, HEAD), BF16),
            pltpu.VMEM((RADIX, SLAB, HEAD), BF16),
            pltpu.VMEM((ROWS_Y, SLAB, HEAD), BF16),
            pltpu.VMEM((ROWS_Z, 16, HEAD), BF16),
            pltpu.VMEM((ROWS_Z, 16, HEAD), BF16),
            pltpu.VMEM((HEAD, HEAD), F32),
            pltpu.VMEM((RADIX, HEAD, HEAD), BF16),
            pltpu.VMEM((HEADS, HEAD // HEADS, HEAD), F32),
            pltpu.VMEM((HEADS, HEAD // HEADS, HEAD), F32),
        ] + sems,
        compiler_params=pltpu.CompilerParams(
            collective_id=0, has_side_effects=True, vmem_limit_bytes=32 * 1024 * 1024
        ),
        name="suffix_attention",
    )(trans, carried, queries, values, out_proj)


def solution(mesh):
    placed = (
        P(None, "head"),
        P("seq", "head"),
        P("seq", "head"),
        P("seq", "head"),
        P("head", "seq"),
    )
    return jax.shard_map(
        on_device, mesh=mesh, in_specs=placed, out_specs=P("head", "seq"), check_vma=False
    )
```

```python
import jax
import jax.numpy as jnp
from jax import lax
from jax.experimental import pallas as pl
from jax.experimental.pallas import tpu as pltpu
from jax.sharding import PartitionSpec as P

F32 = jnp.float32
BF16 = jnp.bfloat16
MESH = pl.DeviceIdType.MESH
RADIX = 4
ROWS_Y = 4
ROWS_Z = 16
HEADS = 8
HEAD = 128
ML_ROWS = 16
SLAB = HEAD + ML_ROWS

NN = (((1,), (0,)), ((), ()))
NT = (((1,), (1,)), ((), ()))
TN = (((0,), (0,)), ((), ()))


def dot(a, b, dims=NN):
    return lax.dot_general(a, b, dims, preferred_element_type=F32)


def split(x):
    high = x.astype(BF16)
    return high, (x - high.astype(F32)).astype(BF16)


def dot3(a, b, dims=NN):
    return dot(a[0], b[0], dims) + (dot(a[0], b[1], dims) + dot(a[1], b[0], dims))


def parts3(x):
    first = x.astype(BF16).astype(F32)
    rest = x - first
    second = rest.astype(BF16).astype(F32)
    return first, second, rest - second


def transition_of(house_ref):
    raw = house_ref[...].astype(F32)
    vectors = raw * lax.rsqrt(jnp.sum(raw * raw, axis=1, keepdims=True) + 1e-06)
    count = vectors.shape[0]
    vec = split(vectors)
    rows = lax.broadcasted_iota(jnp.int32, (count, count), 0)
    cols = lax.broadcasted_iota(jnp.int32, (count, count), 1)
    gram = dot3(vec, vec, NT)
    strict = jnp.where(rows < cols, gram, 0.0)
    pair = (rows | 1) == (cols | 1)
    inverse = jnp.where(rows == cols, 2.0, 0.0) - jnp.where(pair, 4.0 * strict, 0.0)
    size = 2
    while 2 * size < count:
        below = (rows & -(2 * size)) == (cols & -(2 * size))
        below = below & ((rows & size) != (cols & size))
        coupling = split(jnp.where(below, strict, 0.0))
        inv = split(inverse)
        inverse = inverse - dot3(split(dot3(inv, coupling)), inv)
        size *= 2
    coupling = split(jnp.where((rows & size) != (cols & size), strict, 0.0))
    inv = split(inverse)
    half = dot3(inv, vec)
    weights = split(half - dot3(inv, split(dot3(coupling, split(half)))))
    return vec, weights, split(identity() - dot3(weights, vec, TN))


def carried_keys(keys_ref, vec, weights):
    keys = keys_ref[...]
    count = keys.shape[0]
    rows = lax.broadcasted_iota(jnp.int32, (count, count), 0)
    cols = lax.broadcasted_iota(jnp.int32, (count, count), 1)
    inner = dot(keys, vec[0], NT) + dot(keys, vec[1], NT)
    inner = split(jnp.where(rows < cols, inner, 0.0))
    return split(keys.astype(F32) - dot3(inner, weights))


def identity():
    rows = lax.broadcasted_iota(jnp.int32, (HEAD, HEAD), 0)
    cols = lax.broadcasted_iota(jnp.int32, (HEAD, HEAD), 1)
    return jnp.where(rows == cols, 1.0, 0.0)


def chain(buf, last):
    products = [None] * RADIX
    running = (buf[RADIX - 1, 0], buf[RADIX - 1, 1])
    products[RADIX - 1] = running[0].astype(F32) + running[1].astype(F32)
    for i in range(RADIX - 2, last - 1, -1):
        products[i] = dot3(running, (buf[i, 0], buf[i, 1]))
        running = split(products[i])
    return products, running


def chosen(products, position):
    out = identity()
    for i in range(RADIX - 1):
        out = jnp.where(position == i, products[i + 1], out)
    return out


def stat_rows(peak, total, rows):
    ids = lax.broadcasted_iota(jnp.int32, (rows, HEAD), 0)
    out = jnp.zeros((rows, HEAD), F32)
    for i, part in enumerate(parts3(peak) + parts3(total)):
        out = jnp.where(ids == i, part, out)
    return out


def far_first(count):
    return sorted(range(1, count), key=lambda k: -min(k, count - k))


def path_kernel(
    q_ref, keys_ref, v_ref, house_ref, w_ref, o_ref,
    buf_a, buf_b, buf_y, slab_out, slab_in, part_out, part_in, att_z, att_y, weight,
    sem_a, sem_b, sem_c, sem_y, sem_w, sem_sy, sem_sz, sem_gz, sem_gy,
):
    seq = lax.axis_index("seq")
    head = lax.axis_index("head")
    y = lax.div(seq, ROWS_Z)
    z = lax.rem(seq, ROWS_Z)
    a = lax.div(z, RADIX)
    p = lax.rem(z, RADIX)
    pair_head = lax.rem(lax.div(z, 2) - head + HEADS, HEADS)
    stays = pair_head == head
    started = []

    def y_peer(k):
        other = lax.rem(y + k, ROWS_Y)
        return other, (other * ROWS_Z + z, head)

    def z_peer(k):
        other = lax.rem(z + k, ROWS_Z)
        return other, (y * ROWS_Z + other, head)

    def a_peer(k):
        other = lax.rem(a + k, RADIX)
        return other, (y * ROWS_Z + other * RADIX + p, head)

    def p_peer(k):
        other = lax.rem(p + k, RADIX)
        return other, (y * ROWS_Z + a * RADIX + other, head)

    def head_peer(k):
        other = lax.rem(head + k, HEADS)
        return other, (seq, other)

    def merge_peer(k):
        other = lax.rem(z + k, ROWS_Z)
        owner = lax.rem(lax.div(other, 2) - head + HEADS, HEADS)
        return 2 * owner + lax.rem(other, 2), (y * ROWS_Z + other, owner)

    def send(source, target, send_sem, recv_sem, device):
        return pltpu.make_async_remote_copy(
            src_ref=source, dst_ref=target, send_sem=send_sem, recv_sem=recv_sem,
            device_id=device, device_id_type=MESH,
        )

    def exchange(peer, count, sems, source, target):
        copies = []
        for k in far_first(count):
            other, device = peer(k)
            copy = send(source(other), target, sems.at[0, k], sems.at[1, k], device)
            copy.start()
            copies.append(copy)
        started.extend(copies)
        return copies

    def arrived(copies):
        for copy in copies:
            copy.wait_recv()

    barrier = pltpu.get_barrier_semaphore()
    peers = 0
    for peer, count in ((z_peer, ROWS_Z), (y_peer, ROWS_Y), (head_peer, HEADS)):
        for k in far_first(count):
            pl.semaphore_signal(barrier, inc=1, device_id=peer(k)[1], device_id_type=MESH)
            peers += 1
    for k in far_first(ROWS_Z):
        source = (y * ROWS_Z + lax.rem(z + k, ROWS_Z), pair_head)
        pl.semaphore_signal(barrier, inc=1, device_id=source, device_id_type=MESH)
        peers += 1

    @pl.when(jnp.logical_not(stays))
    def _():
        pl.semaphore_signal(barrier, inc=1, device_id=(seq, pair_head), device_id_type=MESH)

    vec, weights, trans = transition_of(house_ref)
    buf_a[p, 0] = trans[0]
    buf_a[p, 1] = trans[1]
    pl.semaphore_wait(barrier, peers + 1 - stays.astype(jnp.int32))

    copies = exchange(p_peer, RADIX, sem_a, lambda other: buf_a.at[p], buf_a.at[p])
    weight_copies = exchange(head_peer, HEADS, sem_w, lambda other: w_ref, weight.at[head])
    weight[head] = w_ref[...]
    carried = carried_keys(keys_ref, vec, weights)
    arrived(copies)
    products, full = chain(buf_a, 0)
    buf_b[a, 0] = full[0]
    buf_b[a, 1] = full[1]
    quarter = pl.ds(pl.multiple_of(p * 32, 32), 32)
    slices = exchange(a_peer, RADIX, sem_b, lambda other: buf_b.at[a, :, quarter], buf_b.at[a, :, quarter])
    after = split(chosen(products, p))
    copies = []
    for k, piece in reversed(list(zip(far_first(RADIX), slices))):
        piece.wait_recv()
        source = buf_b.at[lax.rem(a + RADIX - k, RADIX), :, quarter]
        for m in far_first(RADIX):
            copy = send(source, source, sem_c.at[0, k, m], sem_c.at[1, k, m], p_peer(m)[1])
            copy.start()
            copies.append(copy)
    started.extend(copies)
    arrived(copies)
    products, full = chain(buf_b, 0)
    buf_y[y, 0] = full[0]
    buf_y[y, 1] = full[1]
    copies = exchange(y_peer, ROWS_Y, sem_y, lambda other: buf_y.at[y], buf_y.at[y])
    after = split(dot3(split(chosen(products, a)), after))
    arrived(copies)
    products, _ = chain(buf_y, 1)
    suffix = split(dot3(split(chosen(products, y)), after))

    for h in range(RADIX):
        query = q_ref[:, h * HEAD:(h + 1) * HEAD]
        turned = split((dot(query, suffix[0]) + dot(query, suffix[1])) * (HEAD ** -0.5))
        scores = dot3(carried, turned, NT)
        peak = jnp.max(scores, axis=0, keepdims=True)
        expo = jnp.exp(scores - peak)
        total = jnp.sum(expo, axis=0, keepdims=True)
        numer = dot(v_ref[...], expo.astype(BF16), TN)
        slab_out[h, 0:HEAD, :] = numer.astype(BF16)
        slab_out[h, HEAD:SLAB, :] = stat_rows(peak, total, ML_ROWS).astype(BF16)

    copies = exchange(y_peer, ROWS_Y, sem_sy, lambda other: slab_out.at[other], slab_in.at[y])
    slab_in[y] = slab_out[y]
    arrived(copies)
    slabs = [slab_in[i].astype(F32) for i in range(ROWS_Y)]
    peaks = [s[HEAD:HEAD + 1] + s[HEAD + 1:HEAD + 2] + s[HEAD + 2:HEAD + 3] for s in slabs]
    totals = [s[HEAD + 3:HEAD + 4] + s[HEAD + 4:HEAD + 5] + s[HEAD + 5:HEAD + 6] for s in slabs]
    peak = jnp.maximum(jnp.maximum(peaks[0], peaks[1]), jnp.maximum(peaks[2], peaks[3]))
    factors = [jnp.exp(one - peak) for one in peaks]
    total = sum(f * t for f, t in zip(factors, totals))
    numer = sum(f * s[0:HEAD] for f, s in zip(factors, slabs))

    numer = numer.T.reshape(ROWS_Z, 8, HEAD)
    stats = stat_rows(peak, total, HEAD).T.reshape(ROWS_Z, 8, HEAD)
    part_out[...] = jnp.concatenate([numer, stats], axis=1).astype(BF16)
    copies = exchange(merge_peer, ROWS_Z, sem_sz, lambda other: part_out.at[other], part_in.at[z])
    own = 2 * pair_head + lax.rem(z, 2)
    same_z = send(part_out.at[own], part_in.at[z], sem_sz.at[0, 0], sem_sz.at[1, 0], (seq, pair_head))

    @pl.when(stays)
    def _():
        part_in[z] = part_out[own]

    @pl.when(jnp.logical_not(stays))
    def _():
        same_z.start()
        same_z.wait_recv()

    arrived(copies)
    parts = part_in[...].astype(F32)
    stats = parts[:, 8:16]
    peaks = stats[:, :, 0:1] + stats[:, :, 1:2] + stats[:, :, 2:3]
    totals = stats[:, :, 3:4] + stats[:, :, 4:5] + stats[:, :, 5:6]
    factors = jnp.exp(peaks - jnp.max(peaks, axis=0, keepdims=True))
    total = jnp.sum(factors * totals, axis=0)
    numer = jnp.sum(factors * parts[:, 0:8], axis=0)
    mine = pl.ds(pl.multiple_of(pair_head * 16 + lax.rem(z, 2) * 8, 8), 8)
    att_z[mine, :] = numer / total
    arrived(exchange(z_peer, ROWS_Z, sem_gz, lambda other: att_z.at[mine], att_z.at[mine]))
    att_y[y] = att_z[...].astype(BF16)
    arrived(exchange(y_peer, ROWS_Y, sem_gy, lambda other: att_y.at[y], att_y.at[y]))

    arrived(weight_copies)
    mixed = jnp.zeros(o_ref.shape, F32)
    for g in range(HEADS):
        rows = slice(g * 16, (g + 1) * 16)
        attention = jnp.concatenate([att_y[i, rows, :] for i in range(ROWS_Y)], axis=1)
        mixed = mixed + dot(attention, weight[g], NT)
    o_ref[...] = mixed.astype(BF16)
    for copy in started:
        copy.wait_send()

    @pl.when(jnp.logical_not(stays))
    def _():
        same_z.wait_send()


def on_device(queries, keys, values, householder, out_proj):
    vmem = pl.BlockSpec(memory_space=pltpu.VMEM)
    rows, columns = out_proj.shape
    return pl.pallas_call(
        path_kernel,
        out_shape=jax.ShapeDtypeStruct((HEAD // HEADS, columns), BF16),
        in_specs=[vmem] * 5,
        out_specs=vmem,
        scratch_shapes=[
            pltpu.VMEM((RADIX, 2, HEAD, HEAD), BF16),
            pltpu.VMEM((RADIX, 2, HEAD, HEAD), BF16),
            pltpu.VMEM((RADIX, 2, HEAD, HEAD), BF16),
            pltpu.VMEM((RADIX, SLAB, HEAD), BF16),
            pltpu.VMEM((ROWS_Y, SLAB, HEAD), BF16),
            pltpu.VMEM((ROWS_Z, 16, HEAD), BF16),
            pltpu.VMEM((ROWS_Z, 16, HEAD), BF16),
            pltpu.VMEM((HEAD, HEAD), F32),
            pltpu.VMEM((RADIX, HEAD, HEAD), BF16),
            pltpu.VMEM((HEADS, columns, rows), BF16),
        ] + [pltpu.SemaphoreType.DMA(n) for n in ((2, 4), (2, 4), (2, 4, 4), (2, 4), (2, 8), (2, 4), (2, 16), (2, 16), (2, 4))],
        compiler_params=pltpu.CompilerParams(
            collective_id=0, has_side_effects=True, vmem_limit_bytes=32 * 1024 * 1024
        ),
        name="path_attention",
    )(queries, keys, values, householder, out_proj.T)


def solution(mesh):
    placed = (
        P(None, "head"),
        P("seq", "head"),
        P("seq", "head"),
        P("seq", "head"),
        P("head", "seq"),
    )
    return jax.shard_map(
        on_device, mesh=mesh, in_specs=placed, out_specs=P("head", "seq"), check_vma=False
    )
```

```python
import jax
import jax.numpy as jnp
from jax import lax
from jax.experimental import pallas as pl
from jax.experimental.pallas import tpu as pltpu
from jax.sharding import PartitionSpec as P

F32 = jnp.float32
BF16 = jnp.bfloat16
MESH = pl.DeviceIdType.MESH
RADIX = 4
ROWS_Y = 4
ROWS_Z = 16
HEADS = 8
HEAD = 128
ML_ROWS = 16
SLAB = HEAD + ML_ROWS

NN = (((1,), (0,)), ((), ()))
NT = (((1,), (1,)), ((), ()))
TN = (((0,), (0,)), ((), ()))


def dot(a, b, dims=NN):
    return lax.dot_general(a, b, dims, preferred_element_type=F32)


def split(x):
    high = x.astype(BF16)
    return high, (x - high.astype(F32)).astype(BF16)


def dot3(a, b, dims=NN):
    left = jnp.concatenate([a[0], a[0], a[1]], axis=dims[0][0][0])
    right = jnp.concatenate([b[0], b[1], b[0]], axis=dims[0][1][0])
    return dot(left, right, dims)


def parts3(x):
    first = x.astype(BF16).astype(F32)
    rest = x - first
    second = rest.astype(BF16).astype(F32)
    return first, second, rest - second


def transition_of(house_ref):
    raw = house_ref[...].astype(F32)
    vectors = raw * lax.rsqrt(jnp.sum(raw * raw, axis=1, keepdims=True) + 1e-06)
    count = vectors.shape[0]
    vec = split(vectors)
    rows = lax.broadcasted_iota(jnp.int32, (count, count), 0)
    cols = lax.broadcasted_iota(jnp.int32, (count, count), 1)
    gram = dot3(vec, vec, NT)
    strict = jnp.where(rows < cols, gram, 0.0)
    pair = (rows | 1) == (cols | 1)
    inverse = jnp.where(rows == cols, 2.0, 0.0) - jnp.where(pair, 4.0 * strict, 0.0)
    size = 2
    while 2 * size < count:
        below = (rows & -(2 * size)) == (cols & -(2 * size))
        below = below & ((rows & size) != (cols & size))
        coupling = split(jnp.where(below, strict, 0.0))
        inv = split(inverse)
        inverse = inverse - dot3(split(dot3(inv, coupling)), inv)
        size *= 2
    coupling = split(jnp.where((rows & size) != (cols & size), strict, 0.0))
    inv = split(inverse)
    half = dot3(inv, vec)
    weights = split(half - dot3(inv, split(dot3(coupling, split(half)))))
    return vec, weights, split(identity() - dot3(weights, vec, TN))


def carried_keys(keys_ref, vec, weights):
    keys = keys_ref[...]
    count = keys.shape[0]
    rows = lax.broadcasted_iota(jnp.int32, (count, count), 0)
    cols = lax.broadcasted_iota(jnp.int32, (count, count), 1)
    inner = dot(keys, vec[0], NT) + dot(keys, vec[1], NT)
    inner = split(jnp.where(rows < cols, inner, 0.0))
    return split(keys.astype(F32) - dot3(inner, weights))


def identity():
    rows = lax.broadcasted_iota(jnp.int32, (HEAD, HEAD), 0)
    cols = lax.broadcasted_iota(jnp.int32, (HEAD, HEAD), 1)
    return jnp.where(rows == cols, 1.0, 0.0)


def chain(buf, last):
    products = [None] * RADIX
    running = (buf[RADIX - 1, 0], buf[RADIX - 1, 1])
    products[RADIX - 1] = running[0].astype(F32) + running[1].astype(F32)
    for i in range(RADIX - 2, last - 1, -1):
        products[i] = dot3(running, (buf[i, 0], buf[i, 1]))
        running = split(products[i])
    return products, running


def chosen(products, position):
    out = identity()
    for i in range(RADIX - 1):
        out = jnp.where(position == i, products[i + 1], out)
    return out


def stat_rows(peak, total, rows):
    ids = lax.broadcasted_iota(jnp.int32, (rows, HEAD), 0)
    out = jnp.zeros((rows, HEAD), F32)
    for i, part in enumerate(parts3(peak) + parts3(total)):
        out = jnp.where(ids == i, part, out)
    return out


def far_first(count):
    return sorted(range(1, count), key=lambda k: -min(k, count - k))


def path_kernel(
    q_ref, keys_ref, v_ref, house_ref, w_ref, o_ref,
    buf_a, buf_b, buf_y, slab_out, slab_in, part_out, part_in, att_z, att_y, weight,
    sem_a, sem_b, sem_c, sem_y, sem_w, sem_sy, sem_sz, sem_gz, sem_gy,
):
    seq = lax.axis_index("seq")
    head = lax.axis_index("head")
    y = lax.div(seq, ROWS_Z)
    z = lax.rem(seq, ROWS_Z)
    a = lax.div(z, RADIX)
    p = lax.rem(z, RADIX)
    pair_head = lax.rem(lax.div(z, 2) - head + HEADS, HEADS)
    stays = pair_head == head
    started = []

    def y_peer(k):
        other = lax.rem(y + k, ROWS_Y)
        return other, (other * ROWS_Z + z, head)

    def z_peer(k):
        other = lax.rem(z + k, ROWS_Z)
        return other, (y * ROWS_Z + other, head)

    def a_peer(k):
        other = lax.rem(a + k, RADIX)
        return other, (y * ROWS_Z + other * RADIX + p, head)

    def p_peer(k):
        other = lax.rem(p + k, RADIX)
        return other, (y * ROWS_Z + a * RADIX + other, head)

    def head_peer(k):
        other = lax.rem(head + k, HEADS)
        return other, (seq, other)

    def merge_peer(k):
        other = lax.rem(z + k, ROWS_Z)
        owner = lax.rem(lax.div(other, 2) - head + HEADS, HEADS)
        return 2 * owner + lax.rem(other, 2), (y * ROWS_Z + other, owner)

    def send(source, target, send_sem, recv_sem, device):
        return pltpu.make_async_remote_copy(
            src_ref=source, dst_ref=target, send_sem=send_sem, recv_sem=recv_sem,
            device_id=device, device_id_type=MESH,
        )

    def exchange(peer, count, sems, source, target):
        copies = []
        for k in far_first(count):
            other, device = peer(k)
            copy = send(source(other), target, sems.at[0, k], sems.at[1, k], device)
            copy.start()
            copies.append(copy)
        started.extend(copies)
        return copies

    def arrived(copies):
        for copy in copies:
            copy.wait_recv()

    barrier = pltpu.get_barrier_semaphore()
    peers = 0
    for peer, count in ((z_peer, ROWS_Z), (y_peer, ROWS_Y), (head_peer, HEADS)):
        for k in far_first(count):
            pl.semaphore_signal(barrier, inc=1, device_id=peer(k)[1], device_id_type=MESH)
            peers += 1
    for k in far_first(ROWS_Z):
        source = (y * ROWS_Z + lax.rem(z + k, ROWS_Z), pair_head)
        pl.semaphore_signal(barrier, inc=1, device_id=source, device_id_type=MESH)
        peers += 1

    @pl.when(jnp.logical_not(stays))
    def _():
        pl.semaphore_signal(barrier, inc=1, device_id=(seq, pair_head), device_id_type=MESH)

    vec, weights, trans = transition_of(house_ref)
    buf_a[p, 0] = trans[0]
    buf_a[p, 1] = trans[1]
    pl.semaphore_wait(barrier, peers + 1 - stays.astype(jnp.int32))

    copies = exchange(p_peer, RADIX, sem_a, lambda other: buf_a.at[p], buf_a.at[p])
    weight_copies = exchange(head_peer, HEADS, sem_w, lambda other: w_ref, weight.at[head])
    weight[head] = w_ref[...]
    carried = carried_keys(keys_ref, vec, weights)
    arrived(copies)
    products, full = chain(buf_a, 0)
    buf_b[a, 0] = full[0]
    buf_b[a, 1] = full[1]
    quarter = pl.ds(pl.multiple_of(p * 32, 32), 32)
    slices = exchange(a_peer, RADIX, sem_b, lambda other: buf_b.at[a, :, quarter], buf_b.at[a, :, quarter])
    after = split(chosen(products, p))
    copies = []
    for k, piece in reversed(list(zip(far_first(RADIX), slices))):
        piece.wait_recv()
        source = buf_b.at[lax.rem(a + RADIX - k, RADIX), :, quarter]
        for m in far_first(RADIX):
            copy = send(source, source, sem_c.at[0, k, m], sem_c.at[1, k, m], p_peer(m)[1])
            copy.start()
            copies.append(copy)
    started.extend(copies)
    arrived(copies)
    products, full = chain(buf_b, 0)
    buf_y[y, 0] = full[0]
    buf_y[y, 1] = full[1]
    copies = exchange(y_peer, ROWS_Y, sem_y, lambda other: buf_y.at[y], buf_y.at[y])
    after = split(dot3(split(chosen(products, a)), after))
    arrived(copies)
    products, _ = chain(buf_y, 1)
    suffix = split(dot3(split(chosen(products, y)), after))

    copies = []
    for k in far_first(ROWS_Y) + [0]:
        h, device = y_peer(k)
        query = q_ref[:, pl.ds(pl.multiple_of(h * HEAD, HEAD), HEAD)]
        turned = split((dot(query, suffix[0]) + dot(query, suffix[1])) * (HEAD ** -0.5))
        scores = dot3(carried, turned, NT)
        peak = jnp.max(scores, axis=0, keepdims=True)
        expo = jnp.exp(scores - peak)
        total = jnp.sum(expo, axis=0, keepdims=True)
        numer = dot(v_ref[...], expo.astype(BF16), TN).astype(BF16)
        stats = stat_rows(peak, total, ML_ROWS).astype(BF16)
        slab = slab_out.at[h] if k else slab_in.at[y]
        slab[0:HEAD, :] = numer
        slab[HEAD:SLAB, :] = stats
        if k:
            copy = send(slab, slab_in.at[y], sem_sy.at[0, k], sem_sy.at[1, k], device)
            copy.start()
            copies.append(copy)
    started.extend(copies)
    arrived(copies)
    slabs = [slab_in[i].astype(F32) for i in range(ROWS_Y)]
    peaks = [s[HEAD:HEAD + 1] + s[HEAD + 1:HEAD + 2] + s[HEAD + 2:HEAD + 3] for s in slabs]
    totals = [s[HEAD + 3:HEAD + 4] + s[HEAD + 4:HEAD + 5] + s[HEAD + 5:HEAD + 6] for s in slabs]
    peak = jnp.maximum(jnp.maximum(peaks[0], peaks[1]), jnp.maximum(peaks[2], peaks[3]))
    factors = [jnp.exp(one - peak) for one in peaks]
    total = sum(f * t for f, t in zip(factors, totals))
    numer = sum(f * s[0:HEAD] for f, s in zip(factors, slabs))

    numer = numer.T.reshape(ROWS_Z, 8, HEAD)
    stats = stat_rows(peak, total, HEAD).T.reshape(ROWS_Z, 8, HEAD)
    part_out[...] = jnp.concatenate([numer, stats], axis=1).astype(BF16)
    copies = exchange(merge_peer, ROWS_Z, sem_sz, lambda other: part_out.at[other], part_in.at[z])
    own = 2 * pair_head + lax.rem(z, 2)
    same_z = send(part_out.at[own], part_in.at[z], sem_sz.at[0, 0], sem_sz.at[1, 0], (seq, pair_head))

    @pl.when(stays)
    def _():
        part_in[z] = part_out[own]

    @pl.when(jnp.logical_not(stays))
    def _():
        same_z.start()
        same_z.wait_recv()

    arrived(copies)
    parts = part_in[...].astype(F32)
    stats = parts[:, 8:16]
    peaks = stats[:, :, 0:1] + stats[:, :, 1:2] + stats[:, :, 2:3]
    totals = stats[:, :, 3:4] + stats[:, :, 4:5] + stats[:, :, 5:6]
    factors = jnp.exp(peaks - jnp.max(peaks, axis=0, keepdims=True))
    total = jnp.sum(factors * totals, axis=0)
    numer = jnp.sum(factors * parts[:, 0:8], axis=0)
    mine = pl.ds(pl.multiple_of(pair_head * 16 + lax.rem(z, 2) * 8, 8), 8)
    att_z[mine, :] = numer / total
    arrived(exchange(z_peer, ROWS_Z, sem_gz, lambda other: att_z.at[mine], att_z.at[mine]))
    att_y[y] = att_z[...].astype(BF16)
    arrived(exchange(y_peer, ROWS_Y, sem_gy, lambda other: att_y.at[y], att_y.at[y]))

    arrived(weight_copies)
    mixed = jnp.zeros(o_ref.shape, F32)
    for g in range(HEADS):
        rows = slice(g * 16, (g + 1) * 16)
        attention = jnp.concatenate([att_y[i, rows, :] for i in range(ROWS_Y)], axis=1)
        mixed = mixed + dot(attention, weight[g], NT)
    o_ref[...] = mixed.astype(BF16)
    for copy in started:
        copy.wait_send()

    @pl.when(jnp.logical_not(stays))
    def _():
        same_z.wait_send()


def on_device(queries, keys, values, householder, out_proj):
    vmem = pl.BlockSpec(memory_space=pltpu.VMEM)
    rows, columns = out_proj.shape
    return pl.pallas_call(
        path_kernel,
        out_shape=jax.ShapeDtypeStruct((HEAD // HEADS, columns), BF16),
        in_specs=[vmem] * 5,
        out_specs=vmem,
        scratch_shapes=[
            pltpu.VMEM((RADIX, 2, HEAD, HEAD), BF16),
            pltpu.VMEM((RADIX, 2, HEAD, HEAD), BF16),
            pltpu.VMEM((RADIX, 2, HEAD, HEAD), BF16),
            pltpu.VMEM((RADIX, SLAB, HEAD), BF16),
            pltpu.VMEM((ROWS_Y, SLAB, HEAD), BF16),
            pltpu.VMEM((ROWS_Z, 16, HEAD), BF16),
            pltpu.VMEM((ROWS_Z, 16, HEAD), BF16),
            pltpu.VMEM((HEAD, HEAD), F32),
            pltpu.VMEM((RADIX, HEAD, HEAD), BF16),
            pltpu.VMEM((HEADS, columns, rows), BF16),
        ] + [pltpu.SemaphoreType.DMA(n) for n in ((2, 4), (2, 4), (2, 4, 4), (2, 4), (2, 8), (2, 4), (2, 16), (2, 16), (2, 4))],
        compiler_params=pltpu.CompilerParams(
            collective_id=0, has_side_effects=True, vmem_limit_bytes=32 * 1024 * 1024
        ),
        name="path_attention",
    )(queries, keys, values, householder, out_proj.T)


def solution(mesh):
    placed = (
        P(None, "head"),
        P("seq", "head"),
        P("seq", "head"),
        P("seq", "head"),
        P("head", "seq"),
    )
    return jax.shard_map(
        on_device, mesh=mesh, in_specs=placed, out_specs=P("head", "seq"), check_vma=False
    )
```

```python
import jax
import jax.numpy as jnp
from jax import lax
from jax.experimental import pallas as pl
from jax.experimental.pallas import tpu as pltpu
from jax.sharding import PartitionSpec as P

F32 = jnp.float32
BF16 = jnp.bfloat16
MESH = pl.DeviceIdType.MESH
RADIX = 4
ROWS_Y = 4
ROWS_Z = 16
HEADS = 8
HEAD = 128
ML_ROWS = 16
SLAB = HEAD + ML_ROWS

NN = (((1,), (0,)), ((), ()))
NT = (((1,), (1,)), ((), ()))
TN = (((0,), (0,)), ((), ()))


def dot(a, b, dims=NN):
    return lax.dot_general(a, b, dims, preferred_element_type=F32)


def split(x):
    high = x.astype(BF16)
    return high, (x - high.astype(F32)).astype(BF16)


def dot3(a, b, dims=NN):
    left = jnp.concatenate([a[0], a[0], a[1]], axis=dims[0][0][0])
    right = jnp.concatenate([b[0], b[1], b[0]], axis=dims[0][1][0])
    return dot(left, right, dims)


def parts3(x):
    first = x.astype(BF16).astype(F32)
    rest = x - first
    second = rest.astype(BF16).astype(F32)
    return first, second, rest - second


def transition_of(house_ref):
    raw = house_ref[...].astype(F32)
    vectors = raw * lax.rsqrt(jnp.sum(raw * raw, axis=1, keepdims=True) + 1e-06)
    count = vectors.shape[0]
    vec = split(vectors)
    rows = lax.broadcasted_iota(jnp.int32, (count, count), 0)
    cols = lax.broadcasted_iota(jnp.int32, (count, count), 1)
    gram = dot3(vec, vec, NT)
    strict = jnp.where(rows < cols, gram, 0.0)
    pair = (rows | 1) == (cols | 1)
    inverse = jnp.where(rows == cols, 2.0, 0.0) - jnp.where(pair, 4.0 * strict, 0.0)
    size = 2
    while 2 * size < count:
        below = (rows & -(2 * size)) == (cols & -(2 * size))
        below = below & ((rows & size) != (cols & size))
        coupling = split(jnp.where(below, strict, 0.0))
        inv = split(inverse)
        inverse = inverse - dot3(split(dot3(inv, coupling)), inv)
        size *= 2
    coupling = split(jnp.where((rows & size) != (cols & size), strict, 0.0))
    inv = split(inverse)
    half = dot3(inv, vec)
    weights = split(half - dot3(inv, split(dot3(coupling, split(half)))))
    return vec, weights, split(identity() - dot3(weights, vec, TN))


def carried_keys(keys_ref, vec, weights):
    keys = keys_ref[...]
    count = keys.shape[0]
    rows = lax.broadcasted_iota(jnp.int32, (count, count), 0)
    cols = lax.broadcasted_iota(jnp.int32, (count, count), 1)
    inner = dot(keys, vec[0], NT) + dot(keys, vec[1], NT)
    inner = split(jnp.where(rows < cols, inner, 0.0))
    return split(keys.astype(F32) - dot3(inner, weights))


def identity():
    rows = lax.broadcasted_iota(jnp.int32, (HEAD, HEAD), 0)
    cols = lax.broadcasted_iota(jnp.int32, (HEAD, HEAD), 1)
    return jnp.where(rows == cols, 1.0, 0.0)


def chain(buf, last):
    products = [None] * RADIX
    running = (buf[RADIX - 1, 0], buf[RADIX - 1, 1])
    products[RADIX - 1] = running[0].astype(F32) + running[1].astype(F32)
    for i in range(RADIX - 2, last - 1, -1):
        products[i] = dot3(running, (buf[i, 0], buf[i, 1]))
        running = split(products[i])
    return products, running


def chosen(products, position):
    out = identity()
    for i in range(RADIX - 1):
        out = jnp.where(position == i, products[i + 1], out)
    return out


def stat_rows(peak, total, rows):
    ids = lax.broadcasted_iota(jnp.int32, (rows, HEAD), 0)
    out = jnp.zeros((rows, HEAD), F32)
    for i, part in enumerate(parts3(peak) + parts3(total)):
        out = jnp.where(ids == i, part, out)
    return out


def far_first(count):
    return sorted(range(1, count), key=lambda k: -min(k, count - k))


def path_kernel(
    q_ref, keys_ref, v_ref, house_ref, w_ref, o_ref,
    buf_a, buf_b, buf_y, slab_out, slab_in, part_out, part_in, att_z, att_y, weight,
    sem_a, sem_b, sem_c, sem_y, sem_w, sem_sy, sem_sz, sem_gz, sem_gy,
):
    seq = lax.axis_index("seq")
    head = lax.axis_index("head")
    y = lax.div(seq, ROWS_Z)
    z = lax.rem(seq, ROWS_Z)
    a = lax.div(z, RADIX)
    p = lax.rem(z, RADIX)
    pair_head = lax.rem(lax.div(z, 2) - head + HEADS, HEADS)
    stays = pair_head == head
    started = []

    def y_peer(k):
        other = lax.rem(y + k, ROWS_Y)
        return other, (other * ROWS_Z + z, head)

    def z_peer(k):
        other = lax.rem(z + k, ROWS_Z)
        return other, (y * ROWS_Z + other, head)

    def a_peer(k):
        other = lax.rem(a + k, RADIX)
        return other, (y * ROWS_Z + other * RADIX + p, head)

    def p_peer(k):
        other = lax.rem(p + k, RADIX)
        return other, (y * ROWS_Z + a * RADIX + other, head)

    def head_peer(k):
        other = lax.rem(head + k, HEADS)
        return other, (seq, other)

    def merge_peer(k):
        other = lax.rem(z + k, ROWS_Z)
        owner = lax.rem(lax.div(other, 2) - head + HEADS, HEADS)
        return 2 * owner + lax.rem(other, 2), (y * ROWS_Z + other, owner)

    def send(source, target, send_sem, recv_sem, device):
        return pltpu.make_async_remote_copy(
            src_ref=source, dst_ref=target, send_sem=send_sem, recv_sem=recv_sem,
            device_id=device, device_id_type=MESH,
        )

    def exchange(peer, count, sems, source, target):
        copies = []
        for k in far_first(count):
            other, device = peer(k)
            copy = send(source(other), target, sems.at[0, k], sems.at[1, k], device)
            copy.start()
            copies.append(copy)
        started.extend(copies)
        return copies

    def arrived(copies):
        for copy in copies:
            copy.wait_recv()

    barrier = pltpu.get_barrier_semaphore()
    peers = 0
    for peer, count in ((p_peer, RADIX), (a_peer, RADIX), (y_peer, ROWS_Y), (head_peer, HEADS)):
        for k in far_first(count):
            pl.semaphore_signal(barrier, inc=1, device_id=peer(k)[1], device_id_type=MESH)
            peers += 1

    vec, weights, trans = transition_of(house_ref)
    buf_a[p, 0] = trans[0]
    buf_a[p, 1] = trans[1]
    pl.semaphore_wait(barrier, peers)

    copies = exchange(p_peer, RADIX, sem_a, lambda other: buf_a.at[p], buf_a.at[p])
    carried = carried_keys(keys_ref, vec, weights)
    arrived(copies)
    products, full = chain(buf_a, 0)
    buf_b[a, 0] = full[0]
    buf_b[a, 1] = full[1]
    quarter = pl.ds(pl.multiple_of(p * 32, 32), 32)
    slices = exchange(a_peer, RADIX, sem_b, lambda other: buf_b.at[a, :, quarter], buf_b.at[a, :, quarter])
    after = split(chosen(products, p))
    copies = []
    for k, piece in reversed(list(zip(far_first(RADIX), slices))):
        piece.wait_recv()
        source = buf_b.at[lax.rem(a + RADIX - k, RADIX), :, quarter]
        for m in far_first(RADIX):
            copy = send(source, source, sem_c.at[0, k, m], sem_c.at[1, k, m], p_peer(m)[1])
            copy.start()
            copies.append(copy)
    started.extend(copies)
    arrived(copies)
    products, full = chain(buf_b, 0)
    buf_y[y, 0] = full[0]
    buf_y[y, 1] = full[1]
    copies = exchange(y_peer, ROWS_Y, sem_y, lambda other: buf_y.at[y], buf_y.at[y])
    weight_copies = exchange(head_peer, HEADS, sem_w, lambda other: w_ref, weight.at[head])
    weight[head] = w_ref[...]
    after = split(dot3(split(chosen(products, a)), after))
    arrived(copies)
    products, _ = chain(buf_y, 1)
    suffix = split(dot3(split(chosen(products, y)), after))

    copies = []
    for k in far_first(ROWS_Y) + [0]:
        h, device = y_peer(k)
        query = q_ref[:, pl.ds(pl.multiple_of(h * HEAD, HEAD), HEAD)]
        turned = split((dot(query, suffix[0]) + dot(query, suffix[1])) * (HEAD ** -0.5))
        scores = dot3(carried, turned, NT)
        peak = jnp.max(scores, axis=0, keepdims=True)
        expo = jnp.exp(scores - peak)
        total = jnp.sum(expo, axis=0, keepdims=True)
        numer = dot(v_ref[...], expo.astype(BF16), TN).astype(BF16)
        stats = stat_rows(peak, total, ML_ROWS).astype(BF16)
        slab = slab_out.at[h] if k else slab_in.at[y]
        slab[0:HEAD, :] = numer
        slab[HEAD:SLAB, :] = stats
        if k:
            copy = send(slab, slab_in.at[y], sem_sy.at[0, k], sem_sy.at[1, k], device)
            copy.start()
            copies.append(copy)
    started.extend(copies)
    arrived(copies)
    slabs = [slab_in[i].astype(F32) for i in range(ROWS_Y)]
    peaks = [s[HEAD:HEAD + 1] + s[HEAD + 1:HEAD + 2] + s[HEAD + 2:HEAD + 3] for s in slabs]
    totals = [s[HEAD + 3:HEAD + 4] + s[HEAD + 4:HEAD + 5] + s[HEAD + 5:HEAD + 6] for s in slabs]
    peak = jnp.maximum(jnp.maximum(peaks[0], peaks[1]), jnp.maximum(peaks[2], peaks[3]))
    factors = [jnp.exp(one - peak) for one in peaks]
    total = sum(f * t for f, t in zip(factors, totals))
    numer = sum(f * s[0:HEAD] for f, s in zip(factors, slabs))

    numer = numer.T.reshape(ROWS_Z, 8, HEAD)
    stats = stat_rows(peak, total, HEAD).T.reshape(ROWS_Z, 8, HEAD)
    part_out[...] = jnp.concatenate([numer, stats], axis=1).astype(BF16)
    arrived(weight_copies)
    copies = exchange(merge_peer, ROWS_Z, sem_sz, lambda other: part_out.at[other], part_in.at[z])
    own = 2 * pair_head + lax.rem(z, 2)
    same_z = send(part_out.at[own], part_in.at[z], sem_sz.at[0, 0], sem_sz.at[1, 0], (seq, pair_head))

    @pl.when(stays)
    def _():
        part_in[z] = part_out[own]

    @pl.when(jnp.logical_not(stays))
    def _():
        same_z.start()
        same_z.wait_recv()

    arrived(copies)
    parts = part_in[...].astype(F32)
    stats = parts[:, 8:16]
    peaks = stats[:, :, 0:1] + stats[:, :, 1:2] + stats[:, :, 2:3]
    totals = stats[:, :, 3:4] + stats[:, :, 4:5] + stats[:, :, 5:6]
    factors = jnp.exp(peaks - jnp.max(peaks, axis=0, keepdims=True))
    total = jnp.sum(factors * totals, axis=0)
    numer = jnp.sum(factors * parts[:, 0:8], axis=0)
    mine = pl.ds(pl.multiple_of(pair_head * 16 + lax.rem(z, 2) * 8, 8), 8)
    att_z[mine, :] = numer / total
    arrived(exchange(z_peer, ROWS_Z, sem_gz, lambda other: att_z.at[mine], att_z.at[mine]))
    att_y[y] = att_z[...].astype(BF16)
    arrived(exchange(y_peer, ROWS_Y, sem_gy, lambda other: att_y.at[y], att_y.at[y]))

    mixed = jnp.zeros(o_ref.shape, F32)
    for g in range(HEADS):
        rows = slice(g * 16, (g + 1) * 16)
        attention = jnp.concatenate([att_y[i, rows, :] for i in range(ROWS_Y)], axis=1)
        mixed = mixed + dot(attention, weight[g], NT)
    o_ref[...] = mixed.astype(BF16)
    for copy in started:
        copy.wait_send()

    @pl.when(jnp.logical_not(stays))
    def _():
        same_z.wait_send()


def on_device(queries, keys, values, householder, out_proj):
    vmem = pl.BlockSpec(memory_space=pltpu.VMEM)
    rows, columns = out_proj.shape
    return pl.pallas_call(
        path_kernel,
        out_shape=jax.ShapeDtypeStruct((HEAD // HEADS, columns), BF16),
        in_specs=[vmem] * 5,
        out_specs=vmem,
        scratch_shapes=[
            pltpu.VMEM((RADIX, 2, HEAD, HEAD), BF16),
            pltpu.VMEM((RADIX, 2, HEAD, HEAD), BF16),
            pltpu.VMEM((RADIX, 2, HEAD, HEAD), BF16),
            pltpu.VMEM((RADIX, SLAB, HEAD), BF16),
            pltpu.VMEM((ROWS_Y, SLAB, HEAD), BF16),
            pltpu.VMEM((ROWS_Z, 16, HEAD), BF16),
            pltpu.VMEM((ROWS_Z, 16, HEAD), BF16),
            pltpu.VMEM((HEAD, HEAD), F32),
            pltpu.VMEM((RADIX, HEAD, HEAD), BF16),
            pltpu.VMEM((HEADS, columns, rows), BF16),
        ] + [pltpu.SemaphoreType.DMA(n) for n in ((2, 4), (2, 4), (2, 4, 4), (2, 4), (2, 8), (2, 4), (2, 16), (2, 16), (2, 4))],
        compiler_params=pltpu.CompilerParams(
            collective_id=0, has_side_effects=True, vmem_limit_bytes=32 * 1024 * 1024
        ),
        name="path_attention",
    )(queries, keys, values, householder, out_proj.T)


def solution(mesh):
    placed = (
        P(None, "head"),
        P("seq", "head"),
        P("seq", "head"),
        P("seq", "head"),
        P("head", "seq"),
    )
    return jax.shard_map(
        on_device, mesh=mesh, in_specs=placed, out_specs=P("head", "seq"), check_vma=False
    )
```

```python
import jax
import jax.numpy as jnp
from jax import lax
from jax.experimental import pallas as pl
from jax.experimental.pallas import tpu as pltpu
from jax.sharding import PartitionSpec as P

F32 = jnp.float32
BF16 = jnp.bfloat16
MESH = pl.DeviceIdType.MESH
RADIX = 4
ROWS_Y = 4
ROWS_Z = 16
HEADS = 8
HEAD = 128
ML_ROWS = 16
SLAB = HEAD + ML_ROWS

NN = (((1,), (0,)), ((), ()))
NT = (((1,), (1,)), ((), ()))
TN = (((0,), (0,)), ((), ()))


def dot(a, b, dims=NN):
    return lax.dot_general(a, b, dims, preferred_element_type=F32)


def split(x):
    high = x.astype(BF16)
    return high, (x - high.astype(F32)).astype(BF16)


def dot3(a, b, dims=NN):
    left = jnp.concatenate([a[0], a[0], a[1]], axis=dims[0][0][0])
    right = jnp.concatenate([b[0], b[1], b[0]], axis=dims[0][1][0])
    return dot(left, right, dims)


def parts3(x):
    first = x.astype(BF16).astype(F32)
    rest = x - first
    second = rest.astype(BF16).astype(F32)
    return first, second, rest - second


def transition_of(house_ref):
    raw = house_ref[...].astype(F32)
    vectors = raw * lax.rsqrt(jnp.sum(raw * raw, axis=1, keepdims=True) + 1e-06)
    count = vectors.shape[0]
    vec = split(vectors)
    rows = lax.broadcasted_iota(jnp.int32, (count, count), 0)
    cols = lax.broadcasted_iota(jnp.int32, (count, count), 1)
    gram = dot3(vec, vec, NT)
    strict = jnp.where(rows < cols, gram, 0.0)
    pair = (rows | 1) == (cols | 1)
    inverse = jnp.where(rows == cols, 2.0, 0.0) - jnp.where(pair, 4.0 * strict, 0.0)
    size = 2
    while 2 * size < count:
        below = (rows & -(2 * size)) == (cols & -(2 * size))
        below = below & ((rows & size) != (cols & size))
        coupling = split(jnp.where(below, strict, 0.0))
        inv = split(inverse)
        inverse = inverse - dot3(split(dot3(inv, coupling)), inv)
        size *= 2
    coupling = split(jnp.where((rows & size) != (cols & size), strict, 0.0))
    inv = split(inverse)
    half = dot3(inv, vec)
    weights = split(half - dot3(inv, split(dot3(coupling, split(half)))))
    return vec, weights, split(identity() - dot3(weights, vec, TN))


def carried_keys(keys_ref, vec, weights):
    keys = keys_ref[...]
    count = keys.shape[0]
    rows = lax.broadcasted_iota(jnp.int32, (count, count), 0)
    cols = lax.broadcasted_iota(jnp.int32, (count, count), 1)
    inner = dot(keys, vec[0], NT) + dot(keys, vec[1], NT)
    inner = split(jnp.where(rows < cols, inner, 0.0))
    return split(keys.astype(F32) - dot3(inner, weights))


def identity():
    rows = lax.broadcasted_iota(jnp.int32, (HEAD, HEAD), 0)
    cols = lax.broadcasted_iota(jnp.int32, (HEAD, HEAD), 1)
    return jnp.where(rows == cols, 1.0, 0.0)


def chain(buf, last):
    products = [None] * RADIX
    running = (buf[RADIX - 1, 0], buf[RADIX - 1, 1])
    products[RADIX - 1] = running[0].astype(F32) + running[1].astype(F32)
    for i in range(RADIX - 2, last - 1, -1):
        products[i] = dot3(running, (buf[i, 0], buf[i, 1]))
        running = split(products[i])
    return products, running


def chosen(products, position):
    out = identity()
    for i in range(RADIX - 1):
        out = jnp.where(position == i, products[i + 1], out)
    return out


def stat_rows(peak, total, rows):
    ids = lax.broadcasted_iota(jnp.int32, (rows, HEAD), 0)
    out = jnp.zeros((rows, HEAD), F32)
    for i, part in enumerate(parts3(peak) + parts3(total)):
        out = jnp.where(ids == i, part, out)
    return out


def far_first(count):
    return sorted(range(1, count), key=lambda k: -min(k, count - k))


def path_kernel(
    q_ref, keys_ref, v_ref, house_ref, w_ref, o_ref,
    buf_a, buf_b, buf_y, slab_out, slab_in, part_out, part_in, att_z, att_y, weight,
    sem_a, sem_b, sem_c, sem_y, sem_w, sem_sy, sem_sz, sem_gz, sem_gy,
):
    seq = lax.axis_index("seq")
    head = lax.axis_index("head")
    y = lax.div(seq, ROWS_Z)
    z = lax.rem(seq, ROWS_Z)
    a = lax.div(z, RADIX)
    p = lax.rem(z, RADIX)
    pair_head = lax.rem(lax.div(z, 2) - head + HEADS, HEADS)
    stays = pair_head == head
    started = []

    def y_peer(k):
        other = lax.rem(y + k, ROWS_Y)
        return other, (other * ROWS_Z + z, head)

    def z_peer(k):
        other = lax.rem(z + k, ROWS_Z)
        return other, (y * ROWS_Z + other, head)

    def a_peer(k):
        other = lax.rem(a + k, RADIX)
        return other, (y * ROWS_Z + other * RADIX + p, head)

    def p_peer(k):
        other = lax.rem(p + k, RADIX)
        return other, (y * ROWS_Z + a * RADIX + other, head)

    def head_peer(k):
        other = lax.rem(head + k, HEADS)
        return other, (seq, other)

    def merge_peer(k):
        other = lax.rem(z + k, ROWS_Z)
        owner = lax.rem(lax.div(other, 2) - head + HEADS, HEADS)
        return 2 * owner + lax.rem(other, 2), (y * ROWS_Z + other, owner)

    def send(source, target, send_sem, recv_sem, device):
        return pltpu.make_async_remote_copy(
            src_ref=source, dst_ref=target, send_sem=send_sem, recv_sem=recv_sem,
            device_id=device, device_id_type=MESH,
        )

    def exchange(peer, count, sems, source, target):
        copies = []
        for k in far_first(count):
            other, device = peer(k)
            copy = send(source(other), target, sems.at[0, k], sems.at[1, k], device)
            copy.start()
            copies.append(copy)
        started.extend(copies)
        return copies

    def arrived(copies):
        for copy in copies:
            copy.wait_recv()

    barrier = pltpu.get_barrier_semaphore()
    peers = 0
    for peer, count in ((p_peer, RADIX), (a_peer, RADIX), (y_peer, ROWS_Y), (head_peer, HEADS)):
        for k in far_first(count):
            pl.semaphore_signal(barrier, inc=1, device_id=peer(k)[1], device_id_type=MESH)
            peers += 1

    vec, weights, trans = transition_of(house_ref)
    buf_a[p, 0] = trans[0]
    buf_a[p, 1] = trans[1]
    pl.semaphore_wait(barrier, peers)

    copies = exchange(p_peer, RADIX, sem_a, lambda other: buf_a.at[p], buf_a.at[p])
    carried = carried_keys(keys_ref, vec, weights)
    arrived(copies)
    products, full = chain(buf_a, 0)
    buf_b[a, 0] = full[0]
    buf_b[a, 1] = full[1]
    quarter = pl.ds(pl.multiple_of(p * 32, 32), 32)
    slices = exchange(a_peer, RADIX, sem_b, lambda other: buf_b.at[a, :, quarter], buf_b.at[a, :, quarter])
    after = split(chosen(products, p))
    copies = []
    for k, piece in reversed(list(zip(far_first(RADIX), slices))):
        piece.wait_recv()
        source = buf_b.at[lax.rem(a + RADIX - k, RADIX), :, quarter]
        for m in far_first(RADIX):
            copy = send(source, source, sem_c.at[0, k, m], sem_c.at[1, k, m], p_peer(m)[1])
            copy.start()
            copies.append(copy)
    started.extend(copies)
    arrived(copies)
    products, full = chain(buf_b, 0)
    buf_y[y, 0] = full[0]
    buf_y[y, 1] = full[1]
    copies = exchange(y_peer, ROWS_Y, sem_y, lambda other: buf_y.at[y], buf_y.at[y])
    weight_copies = exchange(head_peer, HEADS, sem_w, lambda other: w_ref, weight.at[head])
    weight[head] = w_ref[...]
    after = split(dot3(split(chosen(products, a)), after))
    flipped = v_ref[...].astype(F32).T.astype(BF16)
    arrived(copies)
    products, _ = chain(buf_y, 1)
    suffix = split(dot3(split(chosen(products, y)), after))

    copies = []
    for k in far_first(ROWS_Y) + [0]:
        h, device = y_peer(k)
        query = q_ref[:, pl.ds(pl.multiple_of(h * HEAD, HEAD), HEAD)]
        turned = split((dot(query, suffix[0]) + dot(query, suffix[1])) * (HEAD ** -0.5))
        scores = dot3(carried, turned, NT)
        peak = jnp.max(scores, axis=0, keepdims=True)
        expo = jnp.exp(scores - peak)
        total = jnp.sum(expo, axis=0, keepdims=True)
        numer = dot(flipped, expo.astype(BF16)).astype(BF16)
        stats = stat_rows(peak, total, ML_ROWS).astype(BF16)
        slab = slab_out.at[h] if k else slab_in.at[y]
        slab[0:HEAD, :] = numer
        slab[HEAD:SLAB, :] = stats
        if k:
            copy = send(slab, slab_in.at[y], sem_sy.at[0, k], sem_sy.at[1, k], device)
            copy.start()
            copies.append(copy)
    started.extend(copies)
    arrived(copies)
    slabs = [slab_in[i].astype(F32) for i in range(ROWS_Y)]
    peaks = [s[HEAD:HEAD + 1] + s[HEAD + 1:HEAD + 2] + s[HEAD + 2:HEAD + 3] for s in slabs]
    totals = [s[HEAD + 3:HEAD + 4] + s[HEAD + 4:HEAD + 5] + s[HEAD + 5:HEAD + 6] for s in slabs]
    peak = jnp.maximum(jnp.maximum(peaks[0], peaks[1]), jnp.maximum(peaks[2], peaks[3]))
    factors = [jnp.exp(one - peak) for one in peaks]
    total = sum(f * t for f, t in zip(factors, totals))
    numer = sum(f * s[0:HEAD] for f, s in zip(factors, slabs))

    numer = numer.T.reshape(ROWS_Z, 8, HEAD)
    stats = stat_rows(peak, total, HEAD).T.reshape(ROWS_Z, 8, HEAD)
    part_out[...] = jnp.concatenate([numer, stats], axis=1).astype(BF16)
    arrived(weight_copies)
    copies = exchange(merge_peer, ROWS_Z, sem_sz, lambda other: part_out.at[other], part_in.at[z])
    own = 2 * pair_head + lax.rem(z, 2)
    same_z = send(part_out.at[own], part_in.at[z], sem_sz.at[0, 0], sem_sz.at[1, 0], (seq, pair_head))

    @pl.when(stays)
    def _():
        part_in[z] = part_out[own]

    @pl.when(jnp.logical_not(stays))
    def _():
        same_z.start()
        same_z.wait_recv()

    arrived(copies)
    parts = part_in[...].astype(F32)
    stats = parts[:, 8:16].reshape(ROWS_Z * 8, HEAD).astype(BF16)
    lanes = lax.broadcasted_iota(jnp.int32, (HEAD, 2 * HEAD), 0)
    first = jnp.where(lax.broadcasted_iota(jnp.int32, (HEAD, 2 * HEAD), 1) < HEAD, 0, 3)
    spread = dot(stats, jnp.where((lanes >= first) & (lanes < first + 3), 1.0, 0.0).astype(BF16))
    peaks = spread[:, 0:HEAD].reshape(ROWS_Z, 8, HEAD)
    totals = spread[:, HEAD:2 * HEAD].reshape(ROWS_Z, 8, HEAD)
    factors = jnp.exp(peaks - jnp.max(peaks, axis=0, keepdims=True))
    total = jnp.sum(factors * totals, axis=0)
    numer = jnp.sum(factors * parts[:, 0:8], axis=0)
    mine = pl.ds(pl.multiple_of(pair_head * 16 + lax.rem(z, 2) * 8, 8), 8)
    att_z[mine, :] = numer / total
    arrived(exchange(z_peer, ROWS_Z, sem_gz, lambda other: att_z.at[mine], att_z.at[mine]))
    att_y[y] = att_z[...].astype(BF16)
    arrived(exchange(y_peer, ROWS_Y, sem_gy, lambda other: att_y.at[y], att_y.at[y]))

    mixed = jnp.zeros(o_ref.shape, F32)
    for g in range(HEADS):
        rows = slice(g * 16, (g + 1) * 16)
        attention = jnp.concatenate([att_y[i, rows, :] for i in range(ROWS_Y)], axis=1)
        mixed = mixed + dot(attention, weight[g], NT)
    o_ref[...] = mixed.astype(BF16)
    for copy in started:
        copy.wait_send()

    @pl.when(jnp.logical_not(stays))
    def _():
        same_z.wait_send()


def on_device(queries, keys, values, householder, out_proj):
    vmem = pl.BlockSpec(memory_space=pltpu.VMEM)
    rows, columns = out_proj.shape
    return pl.pallas_call(
        path_kernel,
        out_shape=jax.ShapeDtypeStruct((HEAD // HEADS, columns), BF16),
        in_specs=[vmem] * 5,
        out_specs=vmem,
        scratch_shapes=[
            pltpu.VMEM((RADIX, 2, HEAD, HEAD), BF16),
            pltpu.VMEM((RADIX, 2, HEAD, HEAD), BF16),
            pltpu.VMEM((RADIX, 2, HEAD, HEAD), BF16),
            pltpu.VMEM((RADIX, SLAB, HEAD), BF16),
            pltpu.VMEM((ROWS_Y, SLAB, HEAD), BF16),
            pltpu.VMEM((ROWS_Z, 16, HEAD), BF16),
            pltpu.VMEM((ROWS_Z, 16, HEAD), BF16),
            pltpu.VMEM((HEAD, HEAD), F32),
            pltpu.VMEM((RADIX, HEAD, HEAD), BF16),
            pltpu.VMEM((HEADS, columns, rows), BF16),
        ] + [pltpu.SemaphoreType.DMA(n) for n in ((2, 4), (2, 4), (2, 4, 4), (2, 4), (2, 8), (2, 4), (2, 16), (2, 16), (2, 4))],
        compiler_params=pltpu.CompilerParams(
            collective_id=0, has_side_effects=True, vmem_limit_bytes=32 * 1024 * 1024
        ),
        name="path_attention",
    )(queries, keys, values, householder, out_proj.T)


def solution(mesh):
    placed = (
        P(None, "head"),
        P("seq", "head"),
        P("seq", "head"),
        P("seq", "head"),
        P("head", "seq"),
    )
    return jax.shard_map(
        on_device, mesh=mesh, in_specs=placed, out_specs=P("head", "seq"), check_vma=False
    )
```
